128 devices in a mesh: feat: 32 (over x_lo, z, y), frames: 4 (over x_hi, core).
Axes of the slice: x: 4 (x_hi: 2, x_lo: 2; x = x_hi * 2 + x_lo), y: 4, z: 4, core: 2. Of those that a mesh axis runs over, the one named last changes fastest.
Arguments:
- trajectory: bfloat16 [768, 102400], P('frames', 'feat'), may hold values from -40 to 40, as said below
- segment_ids: int32 [768], replicated, may hold values from 0 to 3, never falling along the last dimension, each value on 1 to 384 neighbouring positions
- lag_frames: int32 [3], replicated, may hold values from 1 to 8
Outputs:
- band_tiles: bfloat16 [3, 102400, 3200], P(None, ('feat', 'frames'))
The draws below stay inside these ranges and needn't reach their ends.
Inputs may be any that keep to these rules, and one draw needn't show every extreme that they name: trajectory values lie in this range.
All inputs are finite; a program needn't handle non-finite values.
Results may differ from the reference program's by a relative error of at most 0.0035.
Values may be sent and summed in bfloat16 or wider, within the bound.
No kernel may reach another device: no remote copies, remote signals or barrier semaphores. Data moves between devices by JAX's collectives and lax.ppermute only.
A program may use at most 128 MiB of HBM per device.

```python
import math
import jax
import jax.numpy as jnp
import numpy as np
from jax import lax

FB = 3200
BAND = 3
SEGS = 4
FRAMES = 768
F = 102400
N_FEAT = 32


def draw_trajectory(key, part):
    key = jax.random.fold_in(key, 11)
    key_level, key_spread, key_noise = jax.random.split(key, 3)
    level = jax.random.uniform(key_level, (F,), jnp.float32, 0.5, 1.5)
    spread = jnp.exp(jax.random.uniform(key_spread, (F,), jnp.float32, math.log(0.5), math.log(2.0)))
    source = jax.random.normal(key_noise, (FRAMES + 7, F), jnp.float32)
    noise = source[0:FRAMES]
    for offset in range(1, 8):
        noise = noise + source[offset:offset + FRAMES]
    noise = noise * (1.0 / math.sqrt(8.0))
    ramp = 0.25 + 1.5 * jnp.arange(FRAMES, dtype=jnp.float32) / FRAMES
    values = level[None, :] * ramp[:, None] + spread[None, :] * noise
    return values.astype(jnp.bfloat16)


def length_profile(count, total, most, lean):
    portions = [(1 << 20) // math.isqrt(rank ** lean) + 1 for rank in range(2, count + 1)]
    rest, counts = total - most - (count - 1), [1] * (count - 1)
    while rest > 0:
        free = [i for i in range(count - 1) if counts[i] < most]
        mass, left = sum([portions[i] for i in free]), rest
        for i in free:
            more = min(most - counts[i], max(1, left * portions[i] // mass), rest)
            counts[i] = counts[i] + more
            rest = rest - more
    return np.array([most] + counts)


def ragged_sizes(key, amount, total, bound, slope):
    if amount == 2:
        one = jax.random.randint(key, (), max(1, total - bound), min(bound, total - 1) + 1)
        return jnp.stack([one, total - one])
    tallies = jnp.asarray(length_profile(amount, total, bound, slope), jnp.int32)
    twos = (amount - 1) // 2
    source_of, receiver = tallies[1:1 + 2 * twos:2], tallies[2:2 + 2 * twos:2]
    slack = jnp.minimum(source_of - 1, bound - receiver)
    passed = jax.random.randint(jax.random.fold_in(key, 1), (twos,), 0, 1 << 20) % (slack + 1)
    tallies = tallies.at[1:1 + 2 * twos:2].set(source_of - passed).at[2:2 + 2 * twos:2].set(receiver + passed)
    return tallies[jax.random.permutation(jax.random.fold_in(key, 2), amount)]


def setup_inputs(seed: int = 0) -> dict:
    key_list = jax.random.split(jax.random.key(seed), 4)
    trajectory = draw_trajectory(jax.random.fold_in(key_list[3], 71), 0)
    segment_ids = jnp.searchsorted(jnp.cumsum(ragged_sizes(key_list[1], SEGS, FRAMES, FRAMES // 2, 2)), jnp.arange(FRAMES), side="right").astype(jnp.int32)
    lag_frames = jax.random.randint(key_list[2], (BAND,), 1, 9).astype(jnp.int32)
    return {"trajectory": trajectory, "segment_ids": segment_ids, "lag_frames": lag_frames}


def reference(trajectory, segment_ids, lag_frames):
    column_mean = jnp.sum(trajectory.astype(jnp.float32), axis=0) / FRAMES
    centered = (trajectory.astype(jnp.float32) - column_mean).astype(jnp.bfloat16)
    padded_ids = jnp.concatenate([segment_ids, jnp.full((FRAMES,), -1, jnp.int32)])
    padded_data = jnp.concatenate([centered, jnp.zeros_like(centered)], axis=0)
    results = []
    for offset in range(BAND):
        lag = lag_frames[offset].astype(jnp.int32)
        lagged_ids = lax.dynamic_slice_in_dim(padded_ids, lag, FRAMES, 0)
        paired = (segment_ids == lagged_ids).astype(jnp.bfloat16)
        leading = centered * paired[:, None]
        lagging = lax.dynamic_slice_in_dim(padded_data, lag, FRAMES, 0)
        factor = 0.5 / (FRAMES - lag).astype(jnp.float32)

        def tile(block, leading=leading, lagging=lagging, factor=factor, offset=offset):
            first = (block * FB).astype(jnp.int32)
            second = (((block + offset) % N_FEAT) * FB).astype(jnp.int32)
            lead_here = lax.dynamic_slice_in_dim(leading, first, FB, 1)
            lag_here = lax.dynamic_slice_in_dim(lagging, first, FB, 1)
            lead_there = lax.dynamic_slice_in_dim(leading, second, FB, 1)
            lag_there = lax.dynamic_slice_in_dim(lagging, second, FB, 1)
            total = jnp.dot(lead_here.T, lag_there, preferred_element_type=jnp.float32)
            total = total + jnp.dot(lag_here.T, lead_there, preferred_element_type=jnp.float32)
            return (total * factor).astype(jnp.bfloat16)

        tiles = lax.map(tile, jnp.arange(N_FEAT, dtype=jnp.int32))
        results.append(tiles.reshape(N_FEAT * FB, FB))
    return jnp.stack(results)
```

```python
import functools

import jax
import jax.numpy as jnp
from jax import lax
from jax.experimental import pallas as pl
from jax.experimental.pallas import tpu as pltpu
from jax.sharding import PartitionSpec as P

BAND = 3
AXES = ("feat", "frames")
F32, BF16 = jnp.float32, jnp.bfloat16
CHUNK = 512
VMEM = 60 << 20


def spans(width):
    return [(c, min(CHUNK, width - c)) for c in range(0, width, CHUNK)]


def center(raw, out, start, size):
    frames = raw.shape[0]
    cols = pl.ds(start, size)
    total = jnp.zeros((8, size), F32)
    for r in range(0, frames, 16):
        x = raw[pl.ds(r, 16), cols].astype(F32)
        total = total + (x[:8] + x[8:])
    mean = jnp.sum(total, axis=0, keepdims=True) / frames
    for r in range(0, frames, 16):
        x = raw[pl.ds(r, 16), cols].astype(F32)
        out[pl.ds(r, 16), cols] = (x - mean).astype(BF16)


def load(place, pieces, raw, sems):
    width = raw.shape[1]
    copies = []
    for i, (c, w) in enumerate(spans(width)):
        row = []
        for j, (piece, (flip, first)) in enumerate(zip(pieces, place)):
            rows = piece.shape[0]
            me = lax.bitwise_xor(sems[0], flip)
            at = pl.multiple_of(me * sems[2] + first, 16)
            copy = pltpu.make_async_copy(
                piece.at[:, pl.ds(c, w)],
                raw.at[pl.ds(at, rows), pl.ds(c, w)],
                sems[1].at[i, j],
            )
            copy.start()
            row.append(copy)
        copies.append(row)
    return copies


def multiply(k, y, cent, factor, tile, out, copies, raw, out_sems):
    width = cent.shape[1]
    half = tile.shape[0]
    stores = []
    for i, (c, w) in enumerate(spans(width)):
        for copy in copies[i]:
            copy.wait()
        center(raw, cent, c, w)
        both = jnp.dot(y[...], cent[:, pl.ds(c, w)], preferred_element_type=F32)
        total = both[:half] + both[half:]
        tile[:, pl.ds(c, w)] = (total * factor).astype(BF16)
        store = pltpu.make_async_copy(
            tile.at[:, pl.ds(c, w)], out.at[k, :, pl.ds(c, w)], out_sems.at[i]
        )
        store.start()
        stores.append(store)
    for store in stores:
        store.wait()


def first_kernel(place, frames, n, me_ref, lag_ref, col_ids, row_ids, *refs):
    pieces = refs[:n]
    out, y_out = refs[n], refs[n + 1]
    raw, cent, tile, y0, lagged, in_sems, out_sems = refs[n + 2:]
    f = me_ref[0]
    copies = load(place, pieces, raw, (f, in_sems, frames // 4))
    width = raw.shape[1]
    quarter = width // 4
    for i, (c, w) in enumerate(spans(width)):
        for copy in copies[i]:
            copy.wait()
        center(raw, cent, c, w)
    begin = f * quarter
    aligned = pl.multiple_of((begin // 128) * 128, 128)
    window = lagged.shape[0]
    rest = pl.multiple_of(begin - aligned, 32)
    same = col_ids[...] == row_ids[...]
    shape = (frames, frames)
    gap = lax.broadcasted_iota(jnp.int32, shape, 1) - lax.broadcasted_iota(jnp.int32, shape, 0)
    for k in range(BAND):
        lag = lag_ref[k]
        ahead = jnp.where(jnp.logical_and(same, gap == lag), 1.0, 0.0)
        back = jnp.where(jnp.logical_and(same, gap == -lag), 1.0, 0.0)
        pair = (ahead + back).astype(BF16)
        lagged[...] = lax.dot_general(
            cent[:, pl.ds(aligned, window)], pair, (((0,), (0,)), ((), ())),
            preferred_element_type=F32,
        )
        rows = lagged[pl.ds(rest, quarter), :]
        high = rows.astype(BF16)
        low = (rows - high.astype(F32)).astype(BF16)
        if k == 0:
            y0[pl.ds(0, quarter), :] = high
            y0[pl.ds(quarter, quarter), :] = low
        else:
            y_out[k - 1, pl.ds(0, quarter), :] = high
            y_out[k - 1, pl.ds(quarter, quarter), :] = low
    stores = []
    factor = 0.5 / (frames - lag_ref[0]).astype(F32)
    for i, (c, w) in enumerate(spans(width)):
        both = jnp.dot(y0[...], cent[:, pl.ds(c, w)], preferred_element_type=F32)
        total = both[:quarter] + both[quarter:]
        tile[:, pl.ds(c, w)] = (total * factor).astype(BF16)
        store = pltpu.make_async_copy(
            tile.at[:, pl.ds(c, w)], out.at[0, :, pl.ds(c, w)], out_sems.at[i]
        )
        store.start()
        stores.append(store)
    for store in stores:
        store.wait()


def first_tile(me, lags, ids, placed, frames):
    place, pieces = [p for p, _ in placed], [a for _, a in placed]
    width = pieces[0].shape[1]
    quarter = width // 4
    n, spans_n = len(pieces), len(spans(width))
    window = -(-(quarter + 96) // 128) * 128
    smem = pl.BlockSpec(memory_space=pltpu.SMEM)
    vmem = pl.BlockSpec(memory_space=pltpu.VMEM)
    hbm = pl.BlockSpec(memory_space=pl.ANY)
    return pl.pallas_call(
        functools.partial(first_kernel, place, frames, n),
        out_shape=(
            jax.ShapeDtypeStruct((BAND, quarter, width), BF16),
            jax.ShapeDtypeStruct((BAND - 1, 2 * quarter, frames), BF16),
        ),
        in_specs=[smem, smem, vmem, vmem] + [hbm] * n,
        out_specs=(hbm, vmem),
        scratch_shapes=[
            pltpu.VMEM((frames, width), BF16),
            pltpu.VMEM((frames, width), BF16),
            pltpu.VMEM((quarter, width), BF16),
            pltpu.VMEM((2 * quarter, frames), BF16),
            pltpu.VMEM((window, frames), F32),
            pltpu.SemaphoreType.DMA((spans_n, n)),
            pltpu.SemaphoreType.DMA((spans_n,)),
        ],
        compiler_params=pltpu.CompilerParams(vmem_limit_bytes=VMEM),
        name="first_tile",
    )(me, lags, ids[:, None], ids[None, :], *pieces)


def later_kernel(k, place, frames, n, me_ref, lag_ref, y, *refs):
    pieces = refs[:n]
    out = refs[n + 1]
    raw, cent, tile, in_sems, out_sems = refs[n + 2:]
    copies = load(place, pieces, raw, (me_ref[0], in_sems, frames // 4))
    factor = 0.5 / (frames - lag_ref[k]).astype(F32)
    multiply(k, y.at[0], cent, factor, tile, out, copies, raw, out_sems)


def later_tile(k, me, lags, y, placed, tiles, frames):
    place, pieces = [p for p, _ in placed], [a for _, a in placed]
    width = pieces[0].shape[1]
    quarter = width // 4
    n, spans_n = len(pieces), len(spans(width))
    smem = pl.BlockSpec(memory_space=pltpu.SMEM)
    hbm = pl.BlockSpec(memory_space=pl.ANY)
    y_spec = pl.BlockSpec((1, 2 * quarter, frames), lambda i: (k - 1, 0, 0))
    return pl.pallas_call(
        functools.partial(later_kernel, k, place, frames, n),
        out_shape=jax.ShapeDtypeStruct(tiles.shape, tiles.dtype),
        grid=(1,),
        in_specs=[smem, smem, y_spec] + [hbm] * (n + 1),
        out_specs=hbm,
        scratch_shapes=[
            pltpu.VMEM((frames, width), BF16),
            pltpu.VMEM((frames, width), BF16),
            pltpu.VMEM((quarter, width), BF16),
            pltpu.SemaphoreType.DMA((spans_n, n)),
            pltpu.SemaphoreType.DMA((spans_n,)),
        ],
        input_output_aliases={3 + n: 0},
        compiler_params=pltpu.CompilerParams(vmem_limit_bytes=VMEM),
        name="later_tile",
    )(me, lags, y, *pieces, tiles)


def local(trajectory, segment_ids, lag_frames):
    blocks_n, parts = lax.axis_size("feat"), lax.axis_size("frames")
    frames = segment_ids.shape[0]
    me = lax.axis_index("frames").astype(jnp.int32).reshape(1)

    def move(array, back, flip):
        route = [
            (b * parts + f, ((b - back) % blocks_n) * parts + (f ^ flip))
            for b in range(blocks_n) for f in range(parts)
        ]
        return lax.ppermute(array, AXES, route)

    own = trajectory
    across = move(own, 0, 2)
    next_own = move(own, 1, 0)
    own_core = move(own, 0, 1)
    after_own = move(own, 2, 0)
    across_core = move(across, 0, 1)
    next_across = move(across, 1, 0)
    next_core = move(next_own, 0, 1)
    next_across_core = move(next_across, 0, 1)
    after_across = move(after_own, 0, 2)
    after_core = move(after_own, 0, 1)
    after_across_core = move(after_across, 0, 1)

    def placed(*four):
        return [((flip, 0), a) for flip, a in enumerate(four)]

    tiles, y = first_tile(
        me, lag_frames, segment_ids, placed(own, own_core, across, across_core), frames
    )
    tiles = later_tile(
        1, me, lag_frames, y,
        placed(next_own, next_core, next_across, next_across_core), tiles, frames,
    )
    tiles = later_tile(
        2, me, lag_frames, y,
        placed(after_own, after_core, after_across, after_across_core), tiles, frames,
    )
    return tiles


def solution(mesh):
    return jax.shard_map(
        local,
        mesh=mesh,
        in_specs=(P("frames", "feat"), P(), P()),
        out_specs=P(None, ("feat", "frames"), None),
        check_vma=False,
    )
```

```python
import functools

import jax
import jax.numpy as jnp
from jax import lax
from jax.experimental import pallas as pl
from jax.experimental.pallas import tpu as pltpu
from jax.sharding import PartitionSpec as P

BAND = 3
AXES = ("feat", "frames")
F32, BF16 = jnp.float32, jnp.bfloat16
CHUNK = 512
SPLIT = 2048
VMEM = 60 << 20


def spans(first, last):
    return [(c, min(CHUNK, last - c)) for c in range(first, last, CHUNK)]


def center(raw, out, cols):
    frames = raw.shape[0]
    total = jnp.zeros((8, cols.size), F32)
    for r in range(0, frames, 16):
        x = raw[pl.ds(r, 16), cols].astype(F32)
        total = total + (x[:8] + x[8:])
    mean = jnp.sum(total, axis=0, keepdims=True) / frames
    for r in range(0, frames, 16):
        x = raw[pl.ds(r, 16), cols].astype(F32)
        out[pl.ds(r, 16), cols] = (x - mean).astype(BF16)


def start_loads(f, places, pieces, raw, sems, first, last):
    part = raw.shape[0] // 4
    copies = []
    for i, (c, w) in enumerate(spans(first, last)):
        row = []
        for flip, base, j in places:
            piece = pieces[j]
            if base <= c < base + piece.shape[1]:
                at = pl.multiple_of(lax.bitwise_xor(f, flip) * part, 16)
                copy = pltpu.make_async_copy(
                    piece.at[:, pl.ds(c - base, w)],
                    raw.at[pl.ds(at, part), pl.ds(c - first, w)],
                    sems.at[i, flip],
                )
                copy.start()
                row.append(copy)
        copies.append(row)
    return copies


def product(k, y, cent, tile, out, factor, c, w, first, sem):
    here = pl.ds(c - first, w)
    total = jnp.dot(y, cent[:, here], preferred_element_type=F32)
    tile[:, here] = (total * factor).astype(BF16)
    store = pltpu.make_async_copy(tile.at[:, here], out.at[k, :, pl.ds(c, w)], sem)
    store.start()
    return store


def first_kernel(places, frames, n, me_ref, lag_ref, col_ids, row_ids, *refs):
    pieces = refs[:n]
    out, y_out = refs[n], refs[n + 1]
    raw, cent, tile, lagged, in_sems, out_sems = refs[n + 2:]
    f = me_ref[0]
    width = raw.shape[1]
    quarter = width // 4
    copies = start_loads(f, places, pieces, raw, in_sems, 0, width)
    for i, (c, w) in enumerate(spans(0, width)):
        for copy in copies[i]:
            copy.wait()
        center(raw, cent, pl.ds(c, w))
    begin = f * quarter
    aligned = pl.multiple_of((begin // 128) * 128, 128)
    window = lagged.shape[0]
    rest = pl.multiple_of(begin - aligned, 32)
    mine = cent[:, pl.ds(aligned, window)].T
    same = col_ids[...] == row_ids[...]
    shape = (frames, frames)
    gap = lax.broadcasted_iota(jnp.int32, shape, 1) - lax.broadcasted_iota(jnp.int32, shape, 0)
    for k in range(BAND):
        lag = lag_ref[k]
        ahead = jnp.where(jnp.logical_and(same, gap == lag), 1.0, 0.0)
        back = jnp.where(jnp.logical_and(same, gap == -lag), 1.0, 0.0)
        pair = (ahead + back).astype(BF16)
        lagged[...] = jnp.dot(mine, pair, preferred_element_type=F32)
        y_out[k] = lagged[pl.ds(rest, quarter), :].astype(BF16)
    factor = 0.5 / (frames - lag_ref[0]).astype(F32)
    stores = [
        product(0, y_out[0], cent, tile, out, factor, c, w, 0, out_sems.at[i])
        for i, (c, w) in enumerate(spans(0, width))
    ]
    for store in stores:
        store.wait()


SMEM_SPEC = pl.BlockSpec(memory_space=pltpu.SMEM)
VMEM_SPEC = pl.BlockSpec(memory_space=pltpu.VMEM)
HBM_SPEC = pl.BlockSpec(memory_space=pl.ANY)


def cost(frames, quarter, columns, extra=0):
    return pl.CostEstimate(
        flops=2 * frames * quarter * (2 * columns + extra),
        bytes_accessed=2 * columns * (frames + quarter),
        transcendentals=0,
    )


def listed(placed):
    places = [(flip, base, j) for j, (flip, base, _) in enumerate(placed)]
    return places, [array for _, _, array in placed]


def first_tile(me, lags, ids, placed, frames):
    places, pieces = listed(placed)
    width = pieces[0].shape[1]
    quarter = width // 4
    n, count = len(pieces), len(spans(0, width))
    window = -(-(quarter + 96) // 128) * 128
    return pl.pallas_call(
        functools.partial(first_kernel, places, frames, n),
        out_shape=(
            jax.ShapeDtypeStruct((BAND, quarter, width), BF16),
            jax.ShapeDtypeStruct((BAND, quarter, frames), BF16),
        ),
        in_specs=[SMEM_SPEC, SMEM_SPEC, VMEM_SPEC, VMEM_SPEC] + [HBM_SPEC] * n,
        out_specs=(HBM_SPEC, VMEM_SPEC),
        scratch_shapes=[
            pltpu.VMEM((frames, width), BF16),
            pltpu.VMEM((frames, width), BF16),
            pltpu.VMEM((quarter, width), BF16),
            pltpu.VMEM((window, frames), F32),
            pltpu.SemaphoreType.DMA((count, 4)),
            pltpu.SemaphoreType.DMA((count,)),
        ],
        compiler_params=pltpu.CompilerParams(vmem_limit_bytes=VMEM),
        cost_estimate=cost(frames, quarter, width, 3 * frames),
        name="first_tile",
    )(me, lags, ids[:, None], ids[None, :], *pieces)


def later_kernel(k, places, frames, n, first, last, me_ref, lag_ref, y, *refs):
    pieces = refs[:n]
    out, token = refs[n + 1], refs[n + 2]
    raw, cent, tile, in_sems, out_sems = refs[n + 3:]
    token[0] = 0
    copies = start_loads(me_ref[0], places, pieces, raw, in_sems, first, last)
    factor = 0.5 / (frames - lag_ref[k]).astype(F32)
    steps = spans(first, last)
    stores = []
    for i in range(len(steps) + 1):
        if i < len(steps):
            c, w = steps[i]
            for copy in copies[i]:
                copy.wait()
            center(raw, cent, pl.ds(c - first, w))
        if i > 0:
            c, w = steps[i - 1]
            stores.append(
                product(k, y[0], cent, tile, out, factor, c, w, first, out_sems.at[i - 1])
            )
    for store in stores:
        store.wait()


def later_tile(k, me, lags, y, placed, tiles, frames, first, last):
    places, pieces = listed(placed)
    columns = last - first
    quarter = tiles.shape[1]
    n, count = len(pieces), len(spans(first, last))
    y_spec = pl.BlockSpec((1, quarter, frames), lambda i: (k, 0, 0))
    return pl.pallas_call(
        functools.partial(later_kernel, k, places, frames, n, first, last),
        out_shape=(
            jax.ShapeDtypeStruct(tiles.shape, tiles.dtype),
            jax.ShapeDtypeStruct((1,), jnp.int32),
        ),
        grid=(1,),
        in_specs=[SMEM_SPEC, SMEM_SPEC, y_spec] + [HBM_SPEC] * (n + 1),
        out_specs=(HBM_SPEC, SMEM_SPEC),
        scratch_shapes=[
            pltpu.VMEM((frames, columns), BF16),
            pltpu.VMEM((frames, columns), BF16),
            pltpu.VMEM((quarter, columns), BF16),
            pltpu.SemaphoreType.DMA((count, 4)),
            pltpu.SemaphoreType.DMA((count,)),
        ],
        input_output_aliases={3 + n: 0},
        compiler_params=pltpu.CompilerParams(vmem_limit_bytes=VMEM),
        cost_estimate=cost(frames, quarter, columns),
        name="later_tile",
    )(me, lags, y, *pieces, tiles)


def after(array, *done):
    return lax.optimization_barrier((array, *done))[0]


def local(trajectory, segment_ids, lag_frames):
    blocks_n, parts = lax.axis_size("feat"), lax.axis_size("frames")
    frames = segment_ids.shape[0]
    width = trajectory.shape[1]
    half = blocks_n // 2
    me = lax.axis_index("frames").astype(jnp.int32).reshape(1)

    def move(array, to):
        route = []
        for b in range(blocks_n):
            for f in range(parts):
                to_b, to_f = to(b, f)
                route.append((b * parts + f, to_b * parts + to_f))
        return lax.ppermute(array, AXES, route)

    def wraps(b, k):
        return b % half >= half - k

    def core(array):
        return move(array, lambda b, f: (b, f ^ 1))

    def ring(array, k):
        return move(array, lambda b, f: (b - b % half + (b - k) % half, f))

    def straight(array, k):
        return move(array, lambda b, f: ((b + half * wraps(b, k)) % blocks_n, f))

    def cross(array, k):
        return move(array, lambda b, f: ((b + half * wraps(b, k)) % blocks_n, f ^ 2))

    own = trajectory
    across = cross(own, 0)
    next_ring = ring(own, 1)
    own_core = core(own)
    after_ring = ring(after(own, next_ring), 2)
    next_across = cross(next_ring, 1)
    next_own = straight(next_ring, 1)
    across_core = core(across)
    tiles, y = first_tile(
        me, lag_frames, segment_ids,
        [(0, 0, own), (1, 0, own_core), (2, 0, across), (3, 0, across_core)], frames,
    )
    next_core = core(next_own)
    next_across_core = core(next_across)
    after_ring = after(after_ring, y)
    after_across_a = cross(after_ring[:, :SPLIT], 2)
    after_across_b = cross(after_ring[:, SPLIT:], 2)
    after_own = straight(after_ring, 2)
    after_core = core(after_own)
    tiles, token = later_tile(
        1, me, lag_frames, y,
        [(0, 0, next_own), (1, 0, next_core), (2, 0, next_across), (3, 0, next_across_core)],
        tiles, frames, 0, width,
    )
    after_across_a = after(after_across_a, token)
    after_across_core_a = core(after_across_a)
    after_across_core_b = core(after_across_b)
    tiles, token = later_tile(
        2, me, lag_frames, y,
        [(0, 0, after_own), (1, 0, after_core), (2, 0, after_across_a), (3, 0, after_across_core_a)],
        tiles, frames, 0, SPLIT,
    )
    tiles, token = later_tile(
        2, me, lag_frames, y,
        [(0, 0, after_own), (1, 0, after_core), (2, SPLIT, after_across_b), (3, SPLIT, after_across_core_b)],
        tiles, frames, SPLIT, width,
    )
    return tiles


def solution(mesh):
    return jax.shard_map(
        local,
        mesh=mesh,
        in_specs=(P("frames", "feat"), P(), P()),
        out_specs=P(None, ("feat", "frames"), None),
        check_vma=False,
    )
```

```python
import functools

import jax
import jax.numpy as jnp
from jax import lax
from jax.experimental import pallas as pl
from jax.experimental.pallas import tpu as pltpu
from jax.sharding import PartitionSpec as P

BAND = 3
AXES = ("feat", "frames")
F32, BF16 = jnp.float32, jnp.bfloat16
CHUNK = 512
VMEM = 32 << 20


def spans(first, last):
    return [(c, min(CHUNK, last - c)) for c in range(first, last, CHUNK)]


def center(sources, out, cols):
    frames = out.shape[0]
    part = sources[0].shape[0]
    groups = [(j, r) for j in range(len(sources)) for r in range(0, part, 16)]
    total = jnp.zeros((8, cols.size), F32)
    for j, r in groups:
        x = sources[j][pl.ds(r, 16), cols].astype(F32)
        total = total + (x[:8] + x[8:])
    mean = jnp.sum(total, axis=0, keepdims=True) / frames
    for j, r in groups:
        x = sources[j][pl.ds(r, 16), cols].astype(F32)
        out[pl.ds(j * part + r, 16), cols] = (x - mean).astype(BF16)


def start_loads(places, pieces, raw, sems, first, last):
    part = raw.shape[0] // 4
    copies = []
    for flip, base, j in places:
        piece = pieces[j]
        begin, end = max(base, first), min(base + piece.shape[1], last)
        copy = pltpu.make_async_copy(
            piece.at[:, pl.ds(begin - base, end - begin)],
            raw.at[pl.ds(flip * part, part), pl.ds(begin - first, end - begin)],
            sems.at[j],
        )
        copy.start()
        copies.append(copy)
    return copies


def product(k, y, cent, tile, out, factor, c, w, first, sem):
    here = pl.ds(c - first, w)
    total = jnp.dot(y, cent[:, here], preferred_element_type=F32)
    tile[:, here] = (total * factor).astype(BF16)
    store = pltpu.make_async_copy(tile.at[:, here], out.at[k, :, pl.ds(c, w)], sem)
    store.start()
    return store


def border(ids, value, frames):
    def halve(_, span):
        low, high = span
        mid = lax.min((low + high) // 2, frames - 1)
        before = jnp.logical_and(low < high, ids[mid] < value)
        after_ = jnp.logical_and(low < high, jnp.logical_not(before))
        return lax.select(before, mid + 1, low), lax.select(after_, mid, high)

    steps = frames.bit_length()
    return lax.fori_loop(0, steps, halve, (jnp.int32(0), jnp.int32(frames)))[0]


def codes(shape, axis, f, borders):
    row = lax.broadcasted_iota(jnp.int32, shape, axis)
    part = max(shape) // 4
    code = row
    for flip in range(4):
        shift = (lax.bitwise_xor(f, flip) - flip) * part
        here = jnp.logical_and(row >= flip * part, row < (flip + 1) * part)
        code = jnp.where(here, row + shift, code)
    frame = code
    for at in borders:
        code = code + jnp.where(frame >= at, 4096, 0)
    return code


def first_kernel(places, frames, n, me_ref, lag_ref, ids_ref, *refs):
    pieces = refs[:n]
    out, y_out = refs[n], refs[n + 1]
    raw, cent, tile, lagged, in_sems, out_sems = refs[n + 2:]
    f = me_ref[0]
    width = raw.shape[1]
    quarter = width // 4
    copies = start_loads(places, pieces, raw, in_sems, 0, width)
    for copy in copies:
        copy.wait()
    for c, w in spans(0, width):
        center([raw], cent, pl.ds(c, w))
    begin = f * quarter
    aligned = pl.multiple_of((begin // 128) * 128, 128)
    window = lagged.shape[0]
    rest = pl.multiple_of(begin - aligned, 32)
    mine = cent[:, pl.ds(aligned, window)].T
    borders = [border(ids_ref, value, frames) for value in (1, 2, 3)]
    gap = codes((1, frames), 1, f, borders) - codes((frames, 1), 0, f, borders)
    for k in range(BAND):
        lag = lag_ref[k]
        ahead = jnp.where(gap == lag, 1.0, 0.0)
        back = jnp.where(gap == -lag, 1.0, 0.0)
        pair = (ahead + back).astype(BF16)
        lagged[...] = jnp.dot(mine, pair, preferred_element_type=F32)
        y_out[k] = lagged[pl.ds(rest, quarter), :].astype(BF16)
    factor = 0.5 / (frames - lag_ref[0]).astype(F32)
    stores = [
        product(0, y_out[0], cent, tile, out, factor, c, w, 0, out_sems.at[i])
        for i, (c, w) in enumerate(spans(0, width))
    ]
    for store in stores:
        store.wait()


SMEM_SPEC = pl.BlockSpec(memory_space=pltpu.SMEM)
VMEM_SPEC = pl.BlockSpec(memory_space=pltpu.VMEM)
HBM_SPEC = pl.BlockSpec(memory_space=pl.ANY)


def cost(frames, quarter, columns, extra=0):
    return pl.CostEstimate(
        flops=2 * frames * quarter * (2 * columns + extra),
        bytes_accessed=2 * columns * (frames + quarter),
        transcendentals=0,
    )


def listed(placed):
    places = [(flip, base, j) for j, (flip, base, _) in enumerate(placed)]
    return places, [array for _, _, array in placed]


def first_tile(me, lags, ids, placed, frames):
    places, pieces = listed(placed)
    width = pieces[0].shape[1]
    quarter = width // 4
    n, count = len(pieces), len(spans(0, width))
    window = -(-(quarter + 96) // 128) * 128
    return pl.pallas_call(
        functools.partial(first_kernel, places, frames, n),
        out_shape=(
            jax.ShapeDtypeStruct((BAND, quarter, width), BF16),
            jax.ShapeDtypeStruct((BAND, quarter, frames), BF16),
        ),
        in_specs=[SMEM_SPEC] * 3 + [HBM_SPEC] * n,
        out_specs=(HBM_SPEC, VMEM_SPEC),
        scratch_shapes=[
            pltpu.VMEM((frames, width), BF16),
            pltpu.VMEM((frames, width), BF16),
            pltpu.VMEM((quarter, width), BF16),
            pltpu.VMEM((window, frames), F32),
            pltpu.SemaphoreType.DMA((n,)),
            pltpu.SemaphoreType.DMA((count,)),
        ],
        compiler_params=pltpu.CompilerParams(vmem_limit_bytes=VMEM),
        cost_estimate=cost(frames, quarter, width, 3 * frames),
        name="first_tile",
    )(me, lags, ids, *pieces)


def later_kernel(k, places, frames, n, first, last, resident, lags, y_in, *refs):
    pieces = refs[:n]
    out = refs[n + 1]
    cent, tile, y, lag_ref, y_sem, lag_sem, out_sems = refs[n + 2:n + 9]
    lag_copy = pltpu.make_async_copy(lags, lag_ref, lag_sem)
    lag_copy.start()
    y_copy = pltpu.make_async_copy(y_in.at[k], y, y_sem)
    y_copy.start()
    if resident:
        sources, copies = pieces, []
    else:
        raw, in_sems = refs[n + 9:]
        sources = [raw]
        copies = start_loads(places, pieces, raw, in_sems, first, last)
    steps = spans(first, last)
    stores = []
    for copy in copies:
        copy.wait()
    y_copy.wait()
    lag_copy.wait()
    factor = 0.5 / (frames - lag_ref[k]).astype(F32)
    for i in range(len(steps) + 1):
        if i < len(steps):
            c, w = steps[i]
            center(sources, cent, pl.ds(c - first, w))
        if i > 0:
            c, w = steps[i - 1]
            stores.append(
                product(k, y[...], cent, tile, out, factor, c, w, first, out_sems.at[i - 1])
            )
    for store in stores:
        store.wait()


def later_tile(k, lags, y, placed, tiles, frames, first, last, resident=False):
    places, pieces = listed(placed)
    columns = last - first
    quarter = tiles.shape[1]
    n, count = len(pieces), len(spans(first, last))
    scratch = [
        pltpu.VMEM((frames, columns), BF16),
        pltpu.VMEM((quarter, columns), BF16),
        pltpu.VMEM((quarter, frames), BF16),
        pltpu.SMEM((BAND,), jnp.int32),
        pltpu.SemaphoreType.DMA,
        pltpu.SemaphoreType.DMA,
        pltpu.SemaphoreType.DMA((count,)),
    ]
    if not resident:
        scratch += [pltpu.VMEM((frames, columns), BF16), pltpu.SemaphoreType.DMA((n,))]
    piece_spec = VMEM_SPEC if resident else HBM_SPEC
    return pl.pallas_call(
        functools.partial(later_kernel, k, places, frames, n, first, last, resident),
        out_shape=jax.ShapeDtypeStruct(tiles.shape, tiles.dtype),
        in_specs=[HBM_SPEC] * 2 + [piece_spec] * n + [HBM_SPEC],
        out_specs=HBM_SPEC,
        scratch_shapes=scratch,
        input_output_aliases={2 + n: 0},
        compiler_params=pltpu.CompilerParams(vmem_limit_bytes=VMEM),
        cost_estimate=cost(frames, quarter, columns),
        name="later_tile",
    )(lags, y, *pieces, tiles)


def after(array, *done):
    return lax.optimization_barrier((array, *done))[0]


def local(trajectory, segment_ids, lag_frames):
    blocks_n, parts = lax.axis_size("feat"), lax.axis_size("frames")
    frames = segment_ids.shape[0]
    width = trajectory.shape[1]
    half = blocks_n // 2
    me = lax.axis_index("frames").astype(jnp.int32).reshape(1)

    def move(array, to):
        route = []
        for b in range(blocks_n):
            for f in range(parts):
                to_b, to_f = to(b, f)
                route.append((b * parts + f, to_b * parts + to_f))
        return lax.ppermute(array, AXES, route)

    def wraps(b, k):
        return b % half >= half - k

    def core(array):
        return move(array, lambda b, f: (b, f ^ 1))

    def ring(array, k):
        return move(array, lambda b, f: (b - b % half + (b - k) % half, f))

    def wrap(array, k):
        route = [
            (b * parts + f, (b + half) % blocks_n * parts + f)
            for b in range(blocks_n) for f in range(parts) if wraps(b, k)
        ]
        return lax.ppermute(array, AXES, route)

    def straight(array, wrapped, k):
        return jnp.where(wraps(lax.axis_index("feat"), k), wrapped, array)

    def cross(array, k):
        return move(array, lambda b, f: ((b + half * wraps(b, k)) % blocks_n, f ^ 2))

    own = trajectory
    own_core = core(own)
    across = cross(own, 0)
    next_ring = ring(own, 1)
    after_ring = ring(after(own, next_ring), 2)
    next_across = cross(next_ring, 1)
    next_wrap = wrap(next_ring, 1)
    across_core = core(across)
    tiles, y = first_tile(
        me, lag_frames, segment_ids,
        [(0, 0, own), (1, 0, own_core), (2, 0, across), (3, 0, across_core)], frames,
    )
    next_across, next_wrap = lax.optimization_barrier((next_across, next_wrap, y))[:2]
    after_ring = after(after_ring, y)
    after_across = cross(after_ring, 2)
    after_wrap = wrap(after_ring, 2)
    next_own = straight(next_ring, next_wrap, 1)
    next_core = core(next_own)
    next_across_core = core(next_across)
    tiles = later_tile(
        1, lag_frames, y,
        [(0, 0, next_own), (1, 0, next_core), (2, 0, next_across), (3, 0, next_across_core)],
        tiles, frames, 0, width,
    )
    after_across, after_wrap, tiles = lax.optimization_barrier((after_across, after_wrap, tiles))
    after_across_core = core(after_across)
    after_own = straight(after_ring, after_wrap, 2)
    after_core = core(after_own)
    return later_tile(
        2, lag_frames, y,
        [(0, 0, after_own), (1, 0, after_core), (2, 0, after_across), (3, 0, after_across_core)],
        tiles, frames, 0, width, True,
    )


def solution(mesh):
    return jax.shard_map(
        local,
        mesh=mesh,
        in_specs=(P("frames", "feat"), P(), P()),
        out_specs=P(None, ("feat", "frames"), None),
        check_vma=False,
    )
```

```python
import functools

import jax
import jax.numpy as jnp
from jax import lax
from jax.experimental import pallas as pl
from jax.experimental.pallas import tpu as pltpu
from jax.sharding import PartitionSpec as P

BAND = 3
AXES = ("feat", "frames")
F32, BF16 = jnp.float32, jnp.bfloat16
CHUNK = 512
VMEM = 32 << 20


def spans(first, last):
    return [(c, min(CHUNK, last - c)) for c in range(first, last, CHUNK)]


def center(sources, out, cols, wrapped=None):
    frames = out.shape[0]
    part = frames // len(sources)
    groups = [(j, r) for j in range(len(sources)) for r in range(0, part, 16)]

    def get(j, r):
        if not isinstance(sources[j], tuple):
            return sources[j][pl.ds(r, 16), cols]
        plain, other = (ref[pl.ds(r, 16), cols] for ref in sources[j])
        return lax.select(wrapped, other, plain)

    total = jnp.zeros((8, cols.size), F32)
    for j, r in groups:
        x = get(j, r)
        if isinstance(sources[j], tuple):
            out[pl.ds(j * part + r, 16), cols] = x
        x = x.astype(F32)
        total = total + (x[:8] + x[8:])
    mean = jnp.sum(total, axis=0, keepdims=True) / frames
    for j, r in groups:
        there = pl.ds(j * part + r, 16)
        x = out[there, cols] if isinstance(sources[j], tuple) else get(j, r)
        out[there, cols] = (x.astype(F32) - mean).astype(BF16)


def start_loads(places, pieces, raw, sems, first, last):
    part = raw.shape[0] // 4
    copies = []
    for flip, base, j in places:
        piece = pieces[j]
        begin, end = max(base, first), min(base + piece.shape[1], last)
        copy = pltpu.make_async_copy(
            piece.at[:, pl.ds(begin - base, end - begin)],
            raw.at[pl.ds(flip * part, part), pl.ds(begin - first, end - begin)],
            sems.at[j],
        )
        copy.start()
        copies.append(copy)
    return copies


def product(k, y, cent, tile, out, factor, c, w, first, sem):
    here = pl.ds(c - first, w)
    total = jnp.dot(y, cent[:, here], preferred_element_type=F32)
    tile[:, here] = (total * factor).astype(BF16)
    store = pltpu.make_async_copy(tile.at[:, here], out.at[k, :, pl.ds(c, w)], sem)
    store.start()
    return store


def border(ids, value, frames):
    def halve(_, span):
        low, high = span
        mid = lax.min((low + high) // 2, frames - 1)
        before = jnp.logical_and(low < high, ids[mid] < value)
        after_ = jnp.logical_and(low < high, jnp.logical_not(before))
        return lax.select(before, mid + 1, low), lax.select(after_, mid, high)

    steps = frames.bit_length()
    return lax.fori_loop(0, steps, halve, (jnp.int32(0), jnp.int32(frames)))[0]


def codes(shape, axis, f, borders):
    row = lax.broadcasted_iota(jnp.int32, shape, axis)
    part = max(shape) // 4
    code = row
    for flip in range(4):
        shift = (lax.bitwise_xor(f, flip) - flip) * part
        here = jnp.logical_and(row >= flip * part, row < (flip + 1) * part)
        code = jnp.where(here, row + shift, code)
    frame = code
    for at in borders:
        code = code + jnp.where(frame >= at, 4096, 0)
    return code


def first_kernel(places, frames, n, me_ref, lag_ref, ids_ref, *refs):
    pieces = refs[:n]
    out, y_out = refs[n], refs[n + 1]
    raw, cent, tile, lagged, in_sems, out_sems = refs[n + 2:]
    f = me_ref[0]
    width = raw.shape[1]
    quarter = width // 4
    copies = start_loads(places, pieces, raw, in_sems, 0, width)
    for copy in copies:
        copy.wait()
    for c, w in spans(0, width):
        center([raw], cent, pl.ds(c, w))
    begin = f * quarter
    aligned = pl.multiple_of((begin // 128) * 128, 128)
    window = lagged.shape[0]
    rest = pl.multiple_of(begin - aligned, 32)
    mine = cent[:, pl.ds(aligned, window)].T
    borders = [border(ids_ref, value, frames) for value in (1, 2, 3)]
    gap = codes((1, frames), 1, f, borders) - codes((frames, 1), 0, f, borders)
    for k in range(BAND):
        lag = lag_ref[k]
        ahead = jnp.where(gap == lag, 1.0, 0.0)
        back = jnp.where(gap == -lag, 1.0, 0.0)
        pair = (ahead + back).astype(BF16)
        lagged[...] = jnp.dot(mine, pair, preferred_element_type=F32)
        y_out[k] = lagged[pl.ds(rest, quarter), :].astype(BF16)
    factor = 0.5 / (frames - lag_ref[0]).astype(F32)
    stores = [
        product(0, y_out[0], cent, tile, out, factor, c, w, 0, out_sems.at[i])
        for i, (c, w) in enumerate(spans(0, width))
    ]
    for store in stores:
        store.wait()


SMEM_SPEC = pl.BlockSpec(memory_space=pltpu.SMEM)
VMEM_SPEC = pl.BlockSpec(memory_space=pltpu.VMEM)
HBM_SPEC = pl.BlockSpec(memory_space=pl.ANY)


def cost(frames, quarter, columns, extra=0):
    return pl.CostEstimate(
        flops=2 * frames * quarter * (2 * columns + extra),
        bytes_accessed=2 * columns * (frames + quarter),
        transcendentals=0,
    )


def listed(placed):
    places = [(flip, base, j) for j, (flip, base, _) in enumerate(placed)]
    return places, [array for _, _, array in placed]


def first_tile(me, lags, ids, placed, frames):
    places, pieces = listed(placed)
    width = pieces[0].shape[1]
    quarter = width // 4
    n, count = len(pieces), len(spans(0, width))
    window = -(-(quarter + 96) // 128) * 128
    return pl.pallas_call(
        functools.partial(first_kernel, places, frames, n),
        out_shape=(
            jax.ShapeDtypeStruct((BAND, quarter, width), BF16),
            jax.ShapeDtypeStruct((BAND, quarter, frames), BF16),
        ),
        in_specs=[SMEM_SPEC] * 3 + [HBM_SPEC] * n,
        out_specs=(HBM_SPEC, VMEM_SPEC),
        scratch_shapes=[
            pltpu.VMEM((frames, width), BF16),
            pltpu.VMEM((frames, width), BF16),
            pltpu.VMEM((quarter, width), BF16),
            pltpu.VMEM((window, frames), F32),
            pltpu.SemaphoreType.DMA((n,)),
            pltpu.SemaphoreType.DMA((count,)),
        ],
        compiler_params=pltpu.CompilerParams(vmem_limit_bytes=VMEM),
        cost_estimate=cost(frames, quarter, width, 3 * frames),
        name="first_tile",
    )(me, lags, ids, *pieces)


def later_kernel(k, frames, flags, y, *refs):
    ring, beside, core_wrap, across, across_core = refs[:5]
    out, cent, tile, flag, flag_sem, out_sems = refs[6:]
    copy = pltpu.make_async_copy(flags, flag, flag_sem)
    copy.start()
    copy.wait()
    wrapped = flag[BAND + k] > 0
    sources = [(ring, beside), (beside, core_wrap), across, across_core]
    factor = 0.5 / (frames - flag[k]).astype(F32)
    steps = spans(0, tile.shape[1])
    stores = []
    for i in range(len(steps) + 1):
        if i < len(steps):
            center(sources, cent, pl.ds(*steps[i]), wrapped)
        if i > 0:
            c, w = steps[i - 1]
            stores.append(product(k, y[k], cent, tile, out, factor, c, w, 0, out_sems.at[i - 1]))
    for store in stores:
        store.wait()


def later_tile(k, flags, y, pieces, tiles, frames):
    quarter, width = tiles.shape[1:]
    n, count = len(pieces), len(spans(0, width))
    return pl.pallas_call(
        functools.partial(later_kernel, k, frames),
        out_shape=jax.ShapeDtypeStruct(tiles.shape, tiles.dtype),
        in_specs=[HBM_SPEC] + [VMEM_SPEC] * (n + 1) + [HBM_SPEC],
        out_specs=HBM_SPEC,
        scratch_shapes=[
            pltpu.VMEM((frames, width), BF16),
            pltpu.VMEM((quarter, width), BF16),
            pltpu.SMEM(flags.shape, jnp.int32),
            pltpu.SemaphoreType.DMA,
            pltpu.SemaphoreType.DMA((count,)),
        ],
        input_output_aliases={2 + n: 0},
        compiler_params=pltpu.CompilerParams(vmem_limit_bytes=VMEM),
        cost_estimate=cost(frames, quarter, width),
        name="later_tile",
    )(flags, y, *pieces, tiles)


def after(array, *done):
    return lax.optimization_barrier((array, *done))[0]


def local(trajectory, segment_ids, lag_frames):
    blocks_n, parts = lax.axis_size("feat"), lax.axis_size("frames")
    frames = segment_ids.shape[0]
    width = trajectory.shape[1]
    half = blocks_n // 2
    me = lax.axis_index("frames").astype(jnp.int32).reshape(1)

    def move(array, to):
        route = []
        for b in range(blocks_n):
            for f in range(parts):
                to_b, to_f = to(b, f)
                route.append((b * parts + f, to_b * parts + to_f))
        return lax.ppermute(array, AXES, route)

    def wraps(b, k):
        return b % half >= half - k

    def core(array):
        return move(array, lambda b, f: (b, f ^ 1))

    def ring(array, k):
        return move(array, lambda b, f: (b - b % half + (b - k) % half, f))

    def beside(array, k):
        return move(array, lambda b, f: ((b + half) % blocks_n, f) if wraps(b, k) else (b, f ^ 1))

    def swap_wrapped(array, k):
        route = [
            (b * parts + f, b * parts + (f ^ 1))
            for b in range(blocks_n) for f in range(parts) if wraps(b, k)
        ]
        return lax.ppermute(array, AXES, route)

    def cross(array, k):
        return move(array, lambda b, f: ((b + half * wraps(b, k)) % blocks_n, f ^ 2))

    own = trajectory
    flags = jnp.concatenate([
        lag_frames,
        jnp.stack([wraps(lax.axis_index("feat"), k) for k in range(BAND)]).astype(jnp.int32),
    ])
    own_core = core(own)
    across = cross(own, 0)
    next_ring = ring(own, 1)
    after_ring = ring(after(own, across), 2)
    across_core = core(across)
    next_across = cross(next_ring, 1)
    next_beside = beside(next_ring, 1)
    tiles, y = first_tile(
        me, lag_frames, segment_ids,
        [(0, 0, own), (1, 0, own_core), (2, 0, across), (3, 0, across_core)], frames,
    )
    after_ring = after(after_ring, y)
    next_across, next_beside = lax.optimization_barrier((next_across, next_beside, y))[:2]
    after_across = cross(after_ring, 2)
    after_beside = beside(after_ring, 2)
    next_across_core = core(next_across)
    next_core_wrap = swap_wrapped(next_beside, 1)
    tiles = later_tile(
        1, flags, y,
        [next_ring, next_beside, next_core_wrap, next_across, next_across_core], tiles, frames,
    )
    after_across, after_beside, tiles = lax.optimization_barrier(
        (after_across, after_beside, tiles)
    )
    after_across_core = core(after_across)
    after_core_wrap = swap_wrapped(after_beside, 2)
    return later_tile(
        2, flags, y,
        [after_ring, after_beside, after_core_wrap, after_across, after_across_core],
        tiles, frames,
    )


def solution(mesh):
    return jax.shard_map(
        local,
        mesh=mesh,
        in_specs=(P("frames", "feat"), P(), P()),
        out_specs=P(None, ("feat", "frames"), None),
        check_vma=False,
    )
```

```python
import functools

import jax
import jax.numpy as jnp
from jax import lax
from jax.experimental import pallas as pl
from jax.experimental.pallas import tpu as pltpu
from jax.sharding import PartitionSpec as P

BAND = 3
AXES = ("feat", "frames")
F32, BF16 = jnp.float32, jnp.bfloat16
CHUNK = 512
VMEM = 32 << 20


def spans(first, last):
    edges = [first, *range(first + CHUNK // 2, last, CHUNK), last]
    return [(a, b - a) for a, b in zip(edges, edges[1:])]


def center(sources, out, cols, wrapped=None):
    frames = out.shape[0]
    part = frames // len(sources)
    groups = [(j, r) for j in range(len(sources)) for r in range(0, part, 16)]

    def get(j, r):
        if not isinstance(sources[j], tuple):
            return sources[j][pl.ds(r, 16), cols]
        plain, other = (ref[pl.ds(r, 16), cols] for ref in sources[j])
        return lax.select(wrapped, other, plain)

    total = jnp.zeros((8, cols.size), F32)
    for j, r in groups:
        x = get(j, r)
        if isinstance(sources[j], tuple):
            out[pl.ds(j * part + r, 16), cols] = x
        x = x.astype(F32)
        total = total + (x[:8] + x[8:])
    mean = jnp.sum(total, axis=0, keepdims=True) / frames
    for j, r in groups:
        there = pl.ds(j * part + r, 16)
        x = out[there, cols] if isinstance(sources[j], tuple) else get(j, r)
        out[there, cols] = (x.astype(F32) - mean).astype(BF16)


def start_loads(places, pieces, raw, sems, first, last):
    part = raw.shape[0] // 4
    copies = []
    for flip, base, j in places:
        piece = pieces[j]
        begin, end = max(base, first), min(base + piece.shape[1], last)
        copy = pltpu.make_async_copy(
            piece.at[:, pl.ds(begin - base, end - begin)],
            raw.at[pl.ds(flip * part, part), pl.ds(begin - first, end - begin)],
            sems.at[j],
        )
        copy.start()
        copies.append(copy)
    return copies


def product(k, y, cent, tile, out, factor, c, w, first, sem):
    here = pl.ds(c - first, w)
    total = jnp.dot(y, cent[:, here], preferred_element_type=F32)
    tile[:, here] = (total * factor).astype(BF16)
    store = pltpu.make_async_copy(tile.at[:, here], out.at[k, :, pl.ds(c, w)], sem)
    store.start()
    return store


def border(ids, value, frames):
    def halve(_, span):
        low, high = span
        mid = lax.min((low + high) // 2, frames - 1)
        before = jnp.logical_and(low < high, ids[mid] < value)
        after_ = jnp.logical_and(low < high, jnp.logical_not(before))
        return lax.select(before, mid + 1, low), lax.select(after_, mid, high)

    steps = frames.bit_length()
    return lax.fori_loop(0, steps, halve, (jnp.int32(0), jnp.int32(frames)))[0]


def codes(shape, axis, f, borders):
    row = lax.broadcasted_iota(jnp.int32, shape, axis)
    part = max(shape) // 4
    code = row
    for flip in range(4):
        shift = (lax.bitwise_xor(f, flip) - flip) * part
        here = jnp.logical_and(row >= flip * part, row < (flip + 1) * part)
        code = jnp.where(here, row + shift, code)
    frame = code
    for at in borders:
        code = code + jnp.where(frame >= at, 4096, 0)
    return code


def first_kernel(places, frames, n, me_ref, lag_ref, ids_ref, *refs):
    pieces = refs[:n]
    out, y_out = refs[n], refs[n + 1]
    raw, cent, tile, lagged, in_sems, out_sems = refs[n + 2:]
    f = me_ref[0]
    width = raw.shape[1]
    quarter = width // 4
    copies = start_loads(places, pieces, raw, in_sems, 0, width)
    for copy in copies:
        copy.wait()
    for c, w in spans(0, width):
        center([raw], cent, pl.ds(c, w))
    begin = f * quarter
    aligned = pl.multiple_of((begin // 128) * 128, 128)
    window = lagged.shape[0]
    rest = pl.multiple_of(begin - aligned, 32)
    mine = cent[:, pl.ds(aligned, window)].T
    borders = [border(ids_ref, value, frames) for value in (1, 2, 3)]
    gap = codes((1, frames), 1, f, borders) - codes((frames, 1), 0, f, borders)
    for k in range(BAND):
        lag = lag_ref[k]
        ahead = jnp.where(gap == lag, 1.0, 0.0)
        back = jnp.where(gap == -lag, 1.0, 0.0)
        pair = (ahead + back).astype(BF16)
        lagged[...] = jnp.dot(mine, pair, preferred_element_type=F32)
        y_out[k] = lagged[pl.ds(rest, quarter), :].astype(BF16)
    factor = 0.5 / (frames - lag_ref[0]).astype(F32)
    stores = [
        product(0, y_out[0], cent, tile, out, factor, c, w, 0, out_sems.at[i])
        for i, (c, w) in enumerate(spans(0, width))
    ]
    for store in stores:
        store.wait()


SMEM_SPEC = pl.BlockSpec(memory_space=pltpu.SMEM)
VMEM_SPEC = pl.BlockSpec(memory_space=pltpu.VMEM)
HBM_SPEC = pl.BlockSpec(memory_space=pl.ANY)


def cost(frames, quarter, columns, extra=0):
    return pl.CostEstimate(
        flops=2 * frames * quarter * (2 * columns + extra),
        bytes_accessed=2 * columns * (frames + quarter),
        transcendentals=0,
    )


def listed(placed):
    places = [(flip, base, j) for j, (flip, base, _) in enumerate(placed)]
    return places, [array for _, _, array in placed]


def first_tile(me, lags, ids, placed, frames):
    places, pieces = listed(placed)
    width = pieces[0].shape[1]
    quarter = width // 4
    n, count = len(pieces), len(spans(0, width))
    window = -(-(quarter + 96) // 128) * 128
    return pl.pallas_call(
        functools.partial(first_kernel, places, frames, n),
        out_shape=(
            jax.ShapeDtypeStruct((BAND, quarter, width), BF16),
            jax.ShapeDtypeStruct((BAND, quarter, frames), BF16),
        ),
        in_specs=[SMEM_SPEC] * 3 + [HBM_SPEC] * n,
        out_specs=(HBM_SPEC, VMEM_SPEC),
        scratch_shapes=[
            pltpu.VMEM((frames, width), BF16),
            pltpu.VMEM((frames, width), BF16),
            pltpu.VMEM((quarter, width), BF16),
            pltpu.VMEM((window, frames), F32),
            pltpu.SemaphoreType.DMA((n,)),
            pltpu.SemaphoreType.DMA((count,)),
        ],
        compiler_params=pltpu.CompilerParams(vmem_limit_bytes=VMEM),
        cost_estimate=cost(frames, quarter, width, 3 * frames),
        name="first_tile",
    )(me, lags, ids, *pieces)


def later_kernel(k, frames, flags, y, *refs):
    ring, beside, core_wrap, across, across_core = refs[:5]
    out, cent, tile, flag, flag_sem, out_sems = refs[6:]
    copy = pltpu.make_async_copy(flags, flag, flag_sem)
    copy.start()
    copy.wait()
    wrapped = flag[BAND + k] > 0
    sources = [(ring, beside), (beside, core_wrap), across, across_core]
    factor = 0.5 / (frames - flag[k]).astype(F32)
    steps = spans(0, tile.shape[1])
    stores = []
    for i in range(len(steps) + 1):
        if i < len(steps):
            center(sources, cent, pl.ds(*steps[i]), wrapped)
        if i > 0:
            c, w = steps[i - 1]
            stores.append(product(k, y[k], cent, tile, out, factor, c, w, 0, out_sems.at[i - 1]))
    for store in stores:
        store.wait()


def later_tile(k, flags, y, pieces, tiles, frames):
    quarter, width = tiles.shape[1:]
    n, count = len(pieces), len(spans(0, width))
    return pl.pallas_call(
        functools.partial(later_kernel, k, frames),
        out_shape=jax.ShapeDtypeStruct(tiles.shape, tiles.dtype),
        in_specs=[HBM_SPEC] + [VMEM_SPEC] * (n + 1) + [HBM_SPEC],
        out_specs=HBM_SPEC,
        scratch_shapes=[
            pltpu.VMEM((frames, width), BF16),
            pltpu.VMEM((quarter, width), BF16),
            pltpu.SMEM(flags.shape, jnp.int32),
            pltpu.SemaphoreType.DMA,
            pltpu.SemaphoreType.DMA((count,)),
        ],
        input_output_aliases={2 + n: 0},
        compiler_params=pltpu.CompilerParams(vmem_limit_bytes=VMEM),
        cost_estimate=cost(frames, quarter, width),
        name="later_tile",
    )(flags, y, *pieces, tiles)


def fetch_kernel(n, *refs):
    sems = refs[2 * n]
    copies = [pltpu.make_async_copy(refs[j], refs[n + j], sems.at[j]) for j in range(n)]
    for copy in copies:
        copy.start()
    for copy in copies:
        copy.wait()


def fetch(*arrays):
    n = len(arrays)
    return pl.pallas_call(
        functools.partial(fetch_kernel, n),
        out_shape=tuple(jax.ShapeDtypeStruct(a.shape, a.dtype) for a in arrays),
        in_specs=[HBM_SPEC] * n,
        out_specs=(VMEM_SPEC,) * n,
        scratch_shapes=[pltpu.SemaphoreType.DMA((n,))],
        compiler_params=pltpu.CompilerParams(vmem_limit_bytes=VMEM),
        name="fetch",
    )(*arrays)


def after(array, *done):
    return lax.optimization_barrier((array, *done))[0]


def local(trajectory, segment_ids, lag_frames):
    blocks_n, parts = lax.axis_size("feat"), lax.axis_size("frames")
    frames = segment_ids.shape[0]
    width = trajectory.shape[1]
    half = blocks_n // 2
    me = lax.axis_index("frames").astype(jnp.int32).reshape(1)

    def move(array, to):
        route = []
        for b in range(blocks_n):
            for f in range(parts):
                to_b, to_f = to(b, f)
                route.append((b * parts + f, to_b * parts + to_f))
        return lax.ppermute(array, AXES, route)

    def wraps(b, k):
        return b % half >= half - k

    def core(array):
        return move(array, lambda b, f: (b, f ^ 1))

    def ring(array, k):
        return move(array, lambda b, f: (b - b % half + (b - k) % half, f))

    def beside(array, k):
        return move(array, lambda b, f: ((b + half) % blocks_n, f) if wraps(b, k) else (b, f ^ 1))

    def swap_wrapped(array, k):
        route = [
            (b * parts + f, b * parts + (f ^ 1))
            for b in range(blocks_n) for f in range(parts) if wraps(b, k)
        ]
        return lax.ppermute(array, AXES, route)

    def cross(array, k):
        return move(array, lambda b, f: ((b + half * wraps(b, k)) % blocks_n, f ^ 2))

    own = trajectory
    flags = jnp.concatenate([
        lag_frames,
        jnp.stack([wraps(lax.axis_index("feat"), k) for k in range(BAND)]).astype(jnp.int32),
    ])
    own_core = core(own)
    across = cross(own, 0)
    next_ring = ring(own, 1)
    after_ring = ring(next_ring, 1)
    across_core = core(across)
    next_across = cross(next_ring, 1)
    next_beside = beside(next_ring, 1)
    tiles, y = first_tile(
        me, lag_frames, segment_ids,
        [(0, 0, own), (1, 0, own_core), (2, 0, across), (3, 0, across_core)], frames,
    )
    after_ring = after(after_ring, y)
    next_across, next_beside = lax.optimization_barrier((next_across, next_beside, y))[:2]
    after_across = cross(after_ring, 2)
    after_beside = beside(after_ring, 2)
    next_across_core = core(next_across)
    next_core_wrap = swap_wrapped(next_beside, 1)
    tiles = later_tile(
        1, flags, y,
        [next_ring, next_beside, next_core_wrap, next_across, next_across_core], tiles, frames,
    )
    after_across, after_beside, tiles = lax.optimization_barrier(
        (after_across, after_beside, tiles)
    )
    after_across_core = core(after_across)
    after_core_wrap = swap_wrapped(after_beside, 2)
    after_across, after_beside = fetch(after_across, after_beside)
    return later_tile(
        2, flags, y,
        [after_ring, after_beside, after_core_wrap, after_across, after_across_core],
        tiles, frames,
    )


def solution(mesh):
    return jax.shard_map(
        local,
        mesh=mesh,
        in_specs=(P("frames", "feat"), P(), P()),
        out_specs=P(None, ("feat", "frames"), None),
        check_vma=False,
    )
```

```python
import functools

import jax
import jax.numpy as jnp
from jax import lax
from jax.experimental import pallas as pl
from jax.experimental.pallas import tpu as pltpu
from jax.sharding import PartitionSpec as P

BAND = 3
AXES = ("feat", "frames")
F32, BF16 = jnp.float32, jnp.bfloat16
CHUNK = 512
VMEM = 32 << 20


def spans(first, last):
    edges = [first, *range(first + CHUNK // 2, last, CHUNK), last]
    return [(a, b - a) for a, b in zip(edges, edges[1:])]


def center(sources, out, cols, wrapped=None):
    frames = out.shape[0]
    part = frames // len(sources)
    groups = [(j, r) for j in range(len(sources)) for r in range(0, part, 16)]

    def get(j, r):
        if not isinstance(sources[j], tuple):
            return sources[j][pl.ds(r, 16), cols]
        plain, other = (ref[pl.ds(r, 16), cols] for ref in sources[j])
        return lax.select(wrapped, other, plain)

    total = jnp.zeros((8, cols.size), F32)
    for j, r in groups:
        x = get(j, r)
        if isinstance(sources[j], tuple):
            out[pl.ds(j * part + r, 16), cols] = x
        x = x.astype(F32)
        total = total + (x[:8] + x[8:])
    mean = jnp.sum(total, axis=0, keepdims=True) / frames
    for j, r in groups:
        there = pl.ds(j * part + r, 16)
        x = out[there, cols] if isinstance(sources[j], tuple) else get(j, r)
        out[there, cols] = (x.astype(F32) - mean).astype(BF16)


def start_loads(places, pieces, raw, sems, first, last):
    part = raw.shape[0] // 4
    copies = []
    for flip, base, j in places:
        piece = pieces[j]
        begin, end = max(base, first), min(base + piece.shape[1], last)
        copy = pltpu.make_async_copy(
            piece.at[:, pl.ds(begin - base, end - begin)],
            raw.at[pl.ds(flip * part, part), pl.ds(begin - first, end - begin)],
            sems.at[j],
        )
        copy.start()
        copies.append(copy)
    return copies


def product(k, y, cent, tile, out, factor, c, w, first, sem):
    here = pl.ds(c - first, w)
    total = jnp.dot(y, cent[:, here], preferred_element_type=F32)
    tile[:, here] = (total * factor).astype(BF16)
    store = pltpu.make_async_copy(tile.at[:, here], out.at[k, :, pl.ds(c, w)], sem)
    store.start()
    return store


def border(ids, value, frames):
    def halve(_, span):
        low, high = span
        mid = lax.min((low + high) // 2, frames - 1)
        before = jnp.logical_and(low < high, ids[mid] < value)
        after_ = jnp.logical_and(low < high, jnp.logical_not(before))
        return lax.select(before, mid + 1, low), lax.select(after_, mid, high)

    steps = frames.bit_length()
    return lax.fori_loop(0, steps, halve, (jnp.int32(0), jnp.int32(frames)))[0]


def codes(shape, axis, f, borders):
    row = lax.broadcasted_iota(jnp.int32, shape, axis)
    part = max(shape) // 4
    code = row
    for flip in range(4):
        shift = (lax.bitwise_xor(f, flip) - flip) * part
        here = jnp.logical_and(row >= flip * part, row < (flip + 1) * part)
        code = jnp.where(here, row + shift, code)
    frame = code
    for at in borders:
        code = code + jnp.where(frame >= at, 4096, 0)
    return code


def first_kernel(places, frames, n, me_ref, lag_ref, ids_ref, *refs):
    pieces = refs[:n]
    out, y_out = refs[n], refs[n + 1]
    raw, cent, tile, lagged, in_sems, out_sems = refs[n + 2:]
    f = me_ref[0]
    width = raw.shape[1]
    quarter = width // 4
    copies = start_loads(places, pieces, raw, in_sems, 0, width)
    for copy in copies:
        copy.wait()
    for c, w in spans(0, width):
        center([raw], cent, pl.ds(c, w))
    begin = f * quarter
    aligned = pl.multiple_of((begin // 128) * 128, 128)
    window = lagged.shape[0]
    rest = pl.multiple_of(begin - aligned, 32)
    mine = cent[:, pl.ds(aligned, window)].T
    borders = [border(ids_ref, value, frames) for value in (1, 2, 3)]
    gap = codes((1, frames), 1, f, borders) - codes((frames, 1), 0, f, borders)
    for k in range(BAND):
        lag = lag_ref[k]
        ahead = jnp.where(gap == lag, 1.0, 0.0)
        back = jnp.where(gap == -lag, 1.0, 0.0)
        pair = (ahead + back).astype(BF16)
        lagged[...] = jnp.dot(mine, pair, preferred_element_type=F32)
        y_out[k] = lagged[pl.ds(rest, quarter), :].astype(BF16)
    factor = 0.5 / (frames - lag_ref[0]).astype(F32)
    stores = [
        product(0, y_out[0], cent, tile, out, factor, c, w, 0, out_sems.at[i])
        for i, (c, w) in enumerate(spans(0, width))
    ]
    for store in stores:
        store.wait()


SMEM_SPEC = pl.BlockSpec(memory_space=pltpu.SMEM)
VMEM_SPEC = pl.BlockSpec(memory_space=pltpu.VMEM)
HBM_SPEC = pl.BlockSpec(memory_space=pl.ANY)


def cost(frames, quarter, columns, extra=0):
    return pl.CostEstimate(
        flops=2 * frames * quarter * (2 * columns + extra),
        bytes_accessed=2 * columns * (frames + quarter),
        transcendentals=0,
    )


def listed(placed):
    places = [(flip, base, j) for j, (flip, base, _) in enumerate(placed)]
    return places, [array for _, _, array in placed]


def first_tile(me, lags, ids, placed, frames):
    places, pieces = listed(placed)
    width = pieces[0].shape[1]
    quarter = width // 4
    n, count = len(pieces), len(spans(0, width))
    window = -(-(quarter + 96) // 128) * 128
    return pl.pallas_call(
        functools.partial(first_kernel, places, frames, n),
        out_shape=(
            jax.ShapeDtypeStruct((BAND, quarter, width), BF16),
            jax.ShapeDtypeStruct((BAND, quarter, frames), BF16),
        ),
        in_specs=[SMEM_SPEC] * 3 + [HBM_SPEC] * n,
        out_specs=(HBM_SPEC, VMEM_SPEC),
        scratch_shapes=[
            pltpu.VMEM((frames, width), BF16),
            pltpu.VMEM((frames, width), BF16),
            pltpu.VMEM((quarter, width), BF16),
            pltpu.VMEM((window, frames), F32),
            pltpu.SemaphoreType.DMA((n,)),
            pltpu.SemaphoreType.DMA((count,)),
        ],
        compiler_params=pltpu.CompilerParams(vmem_limit_bytes=VMEM),
        cost_estimate=cost(frames, quarter, width, 3 * frames),
        name="first_tile",
    )(me, lags, ids, *pieces)


def later_kernel(k, frames, flags, y, *refs):
    ring, beside, core_wrap, across, across_core = refs[:5]
    out, cent, tile, flag, flag_sem, out_sems = refs[6:]
    copy = pltpu.make_async_copy(flags, flag, flag_sem)
    copy.start()
    copy.wait()
    wrapped = flag[BAND + k] > 0
    sources = [(ring, beside), (beside, core_wrap), across, across_core]
    factor = 0.5 / (frames - flag[k]).astype(F32)
    steps = spans(0, tile.shape[1])
    stores = []
    for i in range(len(steps) + 1):
        if i < len(steps):
            center(sources, cent, pl.ds(*steps[i]), wrapped)
        if i > 0:
            c, w = steps[i - 1]
            stores.append(product(k, y[k], cent, tile, out, factor, c, w, 0, out_sems.at[i - 1]))
    for store in stores:
        store.wait()


def later_tile(k, flags, y, pieces, tiles, frames):
    quarter, width = tiles.shape[1:]
    n, count = len(pieces), len(spans(0, width))
    return pl.pallas_call(
        functools.partial(later_kernel, k, frames),
        out_shape=jax.ShapeDtypeStruct(tiles.shape, tiles.dtype),
        in_specs=[HBM_SPEC] + [VMEM_SPEC] * (n + 1) + [HBM_SPEC],
        out_specs=HBM_SPEC,
        scratch_shapes=[
            pltpu.VMEM((frames, width), BF16),
            pltpu.VMEM((quarter, width), BF16),
            pltpu.SMEM(flags.shape, jnp.int32),
            pltpu.SemaphoreType.DMA,
            pltpu.SemaphoreType.DMA((count,)),
        ],
        input_output_aliases={2 + n: 0},
        compiler_params=pltpu.CompilerParams(vmem_limit_bytes=VMEM),
        cost_estimate=cost(frames, quarter, width),
        name="later_tile",
    )(flags, y, *pieces, tiles)


def fetch_kernel(n, *refs):
    sems = refs[2 * n]
    copies = [pltpu.make_async_copy(refs[j], refs[n + j], sems.at[j]) for j in range(n)]
    for copy in copies:
        copy.start()
    for copy in copies:
        copy.wait()


def fetch(*arrays):
    n = len(arrays)
    return pl.pallas_call(
        functools.partial(fetch_kernel, n),
        out_shape=tuple(jax.ShapeDtypeStruct(a.shape, a.dtype) for a in arrays),
        in_specs=[HBM_SPEC] * n,
        out_specs=(VMEM_SPEC,) * n,
        scratch_shapes=[pltpu.SemaphoreType.DMA((n,))],
        compiler_params=pltpu.CompilerParams(vmem_limit_bytes=VMEM),
        name="fetch",
    )(*arrays)


def after(array, *done):
    return lax.optimization_barrier((array, *done))[0]


def local(trajectory, segment_ids, lag_frames):
    blocks_n, parts = lax.axis_size("feat"), lax.axis_size("frames")
    frames = segment_ids.shape[0]
    width = trajectory.shape[1]
    half = blocks_n // 2
    me = lax.axis_index("frames").astype(jnp.int32).reshape(1)

    def move(array, to):
        route = []
        for b in range(blocks_n):
            for f in range(parts):
                to_b, to_f = to(b, f)
                route.append((b * parts + f, to_b * parts + to_f))
        return lax.ppermute(array, AXES, route)

    def wraps(b, k):
        return b % half >= half - k

    def core(array):
        return move(array, lambda b, f: (b, f ^ 1))

    def ring(array, k):
        return move(array, lambda b, f: (b - b % half + (b - k) % half, f))

    def beside(array, k):
        return move(array, lambda b, f: ((b + half) % blocks_n, f) if wraps(b, k) else (b, f ^ 1))

    def swap_wrapped(array, k):
        route = [
            (b * parts + f, b * parts + (f ^ 1))
            for b in range(blocks_n) for f in range(parts) if wraps(b, k)
        ]
        return lax.ppermute(array, AXES, route)

    def cross(array, k):
        return move(array, lambda b, f: ((b + half * wraps(b, k)) % blocks_n, f ^ 2))

    own = trajectory
    flags = jnp.concatenate([
        lag_frames,
        jnp.stack([wraps(lax.axis_index("feat"), k) for k in range(BAND)]).astype(jnp.int32),
    ])
    own_core = core(own)
    across = cross(own, 0)
    next_ring = ring(own, 1)
    after_ring = ring(next_ring, 1)
    across_core = core(across)
    next_across = cross(next_ring, 1)
    next_beside = beside(next_ring, 1)
    tiles, y = first_tile(
        me, lag_frames, segment_ids,
        [(0, 0, own), (1, 0, own_core), (2, 0, across), (3, 0, across_core)], frames,
    )
    after_ring = after(after_ring, y)
    next_beside = after(next_beside, y)
    next_across = after(next_across, y)
    after_across = cross(after_ring, 2)
    after_beside = beside(after_ring, 2)
    next_core_wrap = swap_wrapped(next_beside, 1)
    next_across_core = core(next_across)
    tiles = later_tile(
        1, flags, y,
        [next_ring, next_beside, next_core_wrap, next_across, next_across_core], tiles, frames,
    )
    after_across, tiles = lax.optimization_barrier((after_across, tiles))
    after_across_core = core(after_across)
    after_beside, tiles = lax.optimization_barrier((after_beside, tiles))
    after_core_wrap = swap_wrapped(after_beside, 2)
    after_across, after_beside = fetch(after_across, after_beside)
    return later_tile(
        2, flags, y,
        [after_ring, after_beside, after_core_wrap, after_across, after_across_core],
        tiles, frames,
    )


def solution(mesh):
    return jax.shard_map(
        local,
        mesh=mesh,
        in_specs=(P("frames", "feat"), P(), P()),
        out_specs=P(None, ("feat", "frames"), None),
        check_vma=False,
    )
```

```python
import functools

import jax
import jax.numpy as jnp
from jax import lax
from jax.experimental import pallas as pl
from jax.experimental.pallas import tpu as pltpu
from jax.sharding import PartitionSpec as P

BAND = 3
AXES = ("feat", "frames")
F32, BF16 = jnp.float32, jnp.bfloat16
CHUNK = 512
VMEM = 32 << 20


def spans(first, last):
    edges = [first, *range(first + CHUNK // 2, last - 128, CHUNK), last - 128, last]
    return [(a, b - a) for a, b in zip(edges, edges[1:])]


def center(sources, out, cols, wrapped=None):
    frames = out.shape[0]
    part = frames // len(sources)
    groups = [(j, r) for j in range(len(sources)) for r in range(0, part, 16)]

    def get(j, r):
        if not isinstance(sources[j], tuple):
            return sources[j][pl.ds(r, 16), cols]
        plain, other = (ref[pl.ds(r, 16), cols] for ref in sources[j])
        return lax.select(wrapped, other, plain)

    total = jnp.zeros((8, cols.size), F32)
    for j, r in groups:
        x = get(j, r)
        if isinstance(sources[j], tuple):
            out[pl.ds(j * part + r, 16), cols] = x
        x = x.astype(F32)
        total = total + (x[:8] + x[8:])
    mean = jnp.sum(total, axis=0, keepdims=True) / frames
    for j, r in groups:
        there = pl.ds(j * part + r, 16)
        x = out[there, cols] if isinstance(sources[j], tuple) else get(j, r)
        out[there, cols] = (x.astype(F32) - mean).astype(BF16)


def start_loads(places, pieces, raw, sems, first, last):
    part = raw.shape[0] // 4
    copies = []
    for flip, base, j in places:
        piece = pieces[j]
        begin, end = max(base, first), min(base + piece.shape[1], last)
        copy = pltpu.make_async_copy(
            piece.at[:, pl.ds(begin - base, end - begin)],
            raw.at[pl.ds(flip * part, part), pl.ds(begin - first, end - begin)],
            sems.at[j],
        )
        copy.start()
        copies.append(copy)
    return copies


def product(k, y, cent, tile, out, factor, c, w, first, sem):
    here = pl.ds(c - first, w)
    total = jnp.dot(y, cent[:, here], preferred_element_type=F32)
    tile[:, here] = (total * factor).astype(BF16)
    store = pltpu.make_async_copy(tile.at[:, here], out.at[k, :, pl.ds(c, w)], sem)
    store.start()
    return store


def border(ids, value, frames):
    def halve(_, span):
        low, high = span
        mid = lax.min((low + high) // 2, frames - 1)
        before = jnp.logical_and(low < high, ids[mid] < value)
        after_ = jnp.logical_and(low < high, jnp.logical_not(before))
        return lax.select(before, mid + 1, low), lax.select(after_, mid, high)

    steps = frames.bit_length()
    return lax.fori_loop(0, steps, halve, (jnp.int32(0), jnp.int32(frames)))[0]


def codes(shape, axis, f, borders):
    row = lax.broadcasted_iota(jnp.int32, shape, axis)
    part = max(shape) // 4
    code = row
    for flip in range(4):
        shift = (lax.bitwise_xor(f, flip) - flip) * part
        here = jnp.logical_and(row >= flip * part, row < (flip + 1) * part)
        code = jnp.where(here, row + shift, code)
    frame = code
    for at in borders:
        code = code + jnp.where(frame >= at, 4096, 0)
    return code


def first_kernel(places, frames, n, me_ref, lag_ref, ids_ref, *refs):
    pieces = refs[:n]
    out, y_out = refs[n], refs[n + 1]
    raw, cent, tile, lagged, in_sems, out_sems = refs[n + 2:]
    f = me_ref[0]
    width = raw.shape[1]
    quarter = width // 4
    copies = start_loads(places, pieces, raw, in_sems, 0, width)
    for copy in copies:
        copy.wait()
    for c, w in spans(0, width):
        center([raw], cent, pl.ds(c, w))
    begin = f * quarter
    aligned = pl.multiple_of((begin // 128) * 128, 128)
    window = lagged.shape[0]
    rest = pl.multiple_of(begin - aligned, 32)
    mine = cent[:, pl.ds(aligned, window)].T
    borders = [border(ids_ref, value, frames) for value in (1, 2, 3)]
    gap = codes((1, frames), 1, f, borders) - codes((frames, 1), 0, f, borders)
    for k in range(BAND):
        lag = lag_ref[k]
        ahead = jnp.where(gap == lag, 1.0, 0.0)
        back = jnp.where(gap == -lag, 1.0, 0.0)
        pair = (ahead + back).astype(BF16)
        lagged[...] = jnp.dot(mine, pair, preferred_element_type=F32)
        y_out[k] = lagged[pl.ds(rest, quarter), :].astype(BF16)
    factor = 0.5 / (frames - lag_ref[0]).astype(F32)
    stores = [
        product(0, y_out[0], cent, tile, out, factor, c, w, 0, out_sems.at[i])
        for i, (c, w) in enumerate(spans(0, width))
    ]
    for store in stores:
        store.wait()


SMEM_SPEC = pl.BlockSpec(memory_space=pltpu.SMEM)
VMEM_SPEC = pl.BlockSpec(memory_space=pltpu.VMEM)
HBM_SPEC = pl.BlockSpec(memory_space=pl.ANY)


def cost(frames, quarter, columns, extra=0):
    return pl.CostEstimate(
        flops=2 * frames * quarter * (2 * columns + extra),
        bytes_accessed=2 * columns * (frames + quarter),
        transcendentals=0,
    )


def listed(placed):
    places = [(flip, base, j) for j, (flip, base, _) in enumerate(placed)]
    return places, [array for _, _, array in placed]


def first_tile(me, lags, ids, placed, frames):
    places, pieces = listed(placed)
    width = pieces[0].shape[1]
    quarter = width // 4
    n, count = len(pieces), len(spans(0, width))
    window = -(-(quarter + 96) // 128) * 128
    return pl.pallas_call(
        functools.partial(first_kernel, places, frames, n),
        out_shape=(
            jax.ShapeDtypeStruct((BAND, quarter, width), BF16),
            jax.ShapeDtypeStruct((BAND, quarter, frames), BF16),
        ),
        in_specs=[SMEM_SPEC] * 3 + [HBM_SPEC] * n,
        out_specs=(HBM_SPEC, VMEM_SPEC),
        scratch_shapes=[
            pltpu.VMEM((frames, width), BF16),
            pltpu.VMEM((frames, width), BF16),
            pltpu.VMEM((quarter, width), BF16),
            pltpu.VMEM((window, frames), F32),
            pltpu.SemaphoreType.DMA((n,)),
            pltpu.SemaphoreType.DMA((count,)),
        ],
        compiler_params=pltpu.CompilerParams(vmem_limit_bytes=VMEM),
        cost_estimate=cost(frames, quarter, width, 3 * frames),
        name="first_tile",
    )(me, lags, ids, *pieces)


def later_kernel(k, frames, flags, y, *refs):
    ring, beside, core_wrap, across, across_core = refs[:5]
    out, cent, tile, flag, flag_sem, out_sems = refs[6:]
    copy = pltpu.make_async_copy(flags, flag, flag_sem)
    copy.start()
    copy.wait()
    wrapped = flag[BAND + k] > 0
    sources = [(ring, beside), (beside, core_wrap), across, across_core]
    factor = 0.5 / (frames - flag[k]).astype(F32)
    steps = spans(0, tile.shape[1])
    stores = []
    for i in range(len(steps) + 1):
        if i < len(steps):
            center(sources, cent, pl.ds(*steps[i]), wrapped)
        if i > 0:
            c, w = steps[i - 1]
            stores.append(product(k, y[k], cent, tile, out, factor, c, w, 0, out_sems.at[i - 1]))
    for store in stores:
        store.wait()


def later_tile(k, flags, y, pieces, tiles, frames):
    quarter, width = tiles.shape[1:]
    n, count = len(pieces), len(spans(0, width))
    return pl.pallas_call(
        functools.partial(later_kernel, k, frames),
        out_shape=jax.ShapeDtypeStruct(tiles.shape, tiles.dtype),
        in_specs=[HBM_SPEC] + [VMEM_SPEC] * (n + 1) + [HBM_SPEC],
        out_specs=HBM_SPEC,
        scratch_shapes=[
            pltpu.VMEM((frames, width), BF16),
            pltpu.VMEM((quarter, width), BF16),
            pltpu.SMEM(flags.shape, jnp.int32),
            pltpu.SemaphoreType.DMA,
            pltpu.SemaphoreType.DMA((count,)),
        ],
        input_output_aliases={2 + n: 0},
        compiler_params=pltpu.CompilerParams(vmem_limit_bytes=VMEM),
        cost_estimate=cost(frames, quarter, width),
        name="later_tile",
    )(flags, y, *pieces, tiles)


def fetch_kernel(n, *refs):
    sems = refs[2 * n]
    copies = [pltpu.make_async_copy(refs[j], refs[n + j], sems.at[j]) for j in range(n)]
    for copy in copies:
        copy.start()
    for copy in copies:
        copy.wait()


def fetch(*arrays):
    n = len(arrays)
    return pl.pallas_call(
        functools.partial(fetch_kernel, n),
        out_shape=tuple(jax.ShapeDtypeStruct(a.shape, a.dtype) for a in arrays),
        in_specs=[HBM_SPEC] * n,
        out_specs=(VMEM_SPEC,) * n,
        scratch_shapes=[pltpu.SemaphoreType.DMA((n,))],
        compiler_params=pltpu.CompilerParams(vmem_limit_bytes=VMEM),
        name="fetch",
    )(*arrays)


def after(array, *done):
    return lax.optimization_barrier((array, *done))[0]


def local(trajectory, segment_ids, lag_frames):
    blocks_n, parts = lax.axis_size("feat"), lax.axis_size("frames")
    frames = segment_ids.shape[0]
    width = trajectory.shape[1]
    half = blocks_n // 2
    me = lax.axis_index("frames").astype(jnp.int32).reshape(1)

    def move(array, to):
        route = []
        for b in range(blocks_n):
            for f in range(parts):
                to_b, to_f = to(b, f)
                route.append((b * parts + f, to_b * parts + to_f))
        return lax.ppermute(array, AXES, route)

    def wraps(b, k):
        return b % half >= half - k

    def core(array):
        return move(array, lambda b, f: (b, f ^ 1))

    def ring(array, k):
        return move(array, lambda b, f: (b - b % half + (b - k) % half, f))

    def beside(array, k):
        return move(array, lambda b, f: ((b + half) % blocks_n, f) if wraps(b, k) else (b, f ^ 1))

    def swap_wrapped(array, k):
        route = [
            (b * parts + f, b * parts + (f ^ 1))
            for b in range(blocks_n) for f in range(parts) if wraps(b, k)
        ]
        return lax.ppermute(array, AXES, route)

    def cross(array, k):
        return move(array, lambda b, f: ((b + half * wraps(b, k)) % blocks_n, f ^ 2))

    own = trajectory
    flags = jnp.concatenate([
        lag_frames,
        jnp.stack([wraps(lax.axis_index("feat"), k) for k in range(BAND)]).astype(jnp.int32),
    ])
    own_core = core(own)
    across = cross(own, 0)
    next_ring = ring(own, 1)
    after_ring = ring(next_ring, 1)
    across_core = core(across)
    next_across = cross(next_ring, 1)
    next_beside = beside(next_ring, 1)
    tiles, y = first_tile(
        me, lag_frames, segment_ids,
        [(0, 0, own), (1, 0, own_core), (2, 0, across), (3, 0, across_core)], frames,
    )
    after_ring = after(after_ring, y)
    next_beside = after(next_beside, y)
    next_across = after(next_across, y)
    after_across = cross(after_ring, 2)
    after_beside = beside(after_ring, 2)
    next_core_wrap = swap_wrapped(next_beside, 1)
    next_across_core = core(next_across)
    tiles = later_tile(
        1, flags, y,
        [next_ring, next_beside, next_core_wrap, next_across, next_across_core], tiles, frames,
    )
    after_across, tiles = lax.optimization_barrier((after_across, tiles))
    after_across_core = core(after_across)
    after_beside, tiles = lax.optimization_barrier((after_beside, tiles))
    after_core_wrap = swap_wrapped(after_beside, 2)
    after_across, after_beside = fetch(after_across, after_beside)
    return later_tile(
        2, flags, y,
        [after_ring, after_beside, after_core_wrap, after_across, after_across_core],
        tiles, frames,
    )


def solution(mesh):
    return jax.shard_map(
        local,
        mesh=mesh,
        in_specs=(P("frames", "feat"), P(), P()),
        out_specs=P(None, ("feat", "frames"), None),
        check_vma=False,
    )
```
